1024 devices in a mesh: expert: 16 (over z), group: 64 (over x, y, core).
Axes of the slice: x: 4, y: 8, z: 16, core: 2. Of those that a mesh axis runs over, the one named last changes fastest.
Arguments:
- tokens: bfloat16 [4096, 2048], P('expert'), may hold values from -6 to 6
- routes: int32 [4096, 8], P('expert'), may hold values from 0 to 127, as said below
- combine: bfloat16 [4096, 8], P('expert'), may hold values from 0.049804688 to 0.3984375
- gate_weight: bfloat16 [196608, 2048], P(('expert', 'group')), may hold values from -0.125 to 0.125
- up_weight: bfloat16 [196608, 2048], P(('expert', 'group')), may hold values from -0.125 to 0.125
- direction: bfloat16 [196608, 2048], P(('expert', 'group')), may hold values from -0.29882812 to 0.29882812
Outputs:
- tangent_out: bfloat16 [4096, 2048], P('expert')
- curvature: bfloat16 [196608, 2048], P(('expert', 'group'))
The draws below stay inside these ranges and needn't reach their ends.
Inputs may be any that keep to these rules, and one draw needn't show every extreme that they name: `routes`: each token names 8 different experts. In each block of 256 consecutive tokens no expert is named by more than 32 tokens, and some expert is named by exactly 32 tokens in every block.
All inputs are finite; a program needn't handle non-finite values.
Results may differ from the reference program's by a relative error of at most 0.015.
Values may be sent and summed in bfloat16 or wider, within the bound.
No kernel may reach another device: no remote copies, remote signals or barrier semaphores. Data moves between devices by JAX's collectives and lax.ppermute only.
A program may use at most 32 MiB of HBM per device.

```python
import jax
import jax.numpy as jnp
from jax import lax

D = 2048
FF = 1536
TOP = 8
COL_TOK = 256
EXPERTS = 128
SPLIT = 8
UNITS = 192
CAP = 32
TOKENS = 4096


def draw_routes(key, part):
    key = jax.random.fold_in(key, 7)
    key_shift, key_kept, key_order, key_full = jax.random.split(key, 4)
    blocks = TOKENS // COL_TOK
    stride = EXPERTS // TOP
    full_count = COL_TOK // CAP
    offset_base = jax.random.randint(key_shift, (), 0, EXPERTS)
    kept_rows = jax.random.randint(key_kept, (blocks, TOP, full_count), CAP // 2, CAP + 1)
    full_bucket = jax.random.randint(key_full, (blocks, 1, 1), 0, full_count)
    kept_rows = jnp.where(jnp.arange(full_count)[None, None, :] == full_bucket, CAP, kept_rows)
    order_keys = jax.random.split(key_order, blocks * TOP)
    placing = jax.vmap(lambda subkey: jax.random.permutation(subkey, COL_TOK))(order_keys)
    placing = placing.reshape(blocks, TOP, COL_TOK)
    bucket_id = placing // CAP
    within = placing % CAP
    kept_count = jnp.take_along_axis(kept_rows, bucket_id, axis=2)
    bucket_id = jnp.where(within >= kept_count, bucket_id + full_count, bucket_id)
    expert_id = offset_base + jnp.arange(TOP)[None, :, None] * stride + bucket_id
    expert_id = jnp.transpose(expert_id % EXPERTS, (0, 2, 1))
    return expert_id.reshape(TOKENS, TOP).astype(jnp.int32)


def steps_of(rng, extent, cuts, smallest, largest):
    level, own = 1.0, jax.random.fold_in(rng, 6)
    for position, shards_of in cuts:
        heights = jnp.exp(jax.random.uniform(jax.random.fold_in(own, position), (shards_of,), jnp.float32, smallest / len(cuts), largest / len(cuts)))
        level = level * jnp.repeat(heights, extent[position] // shards_of).reshape([-1 if axis == position else 1 for axis in range(len(extent))])
    return level


def bell_draw(rng, shape, width, most, cuts=(), kind=jnp.bfloat16):
    values = jax.random.normal(rng, shape, jnp.float32) * width
    if len(cuts) > 0:
        values = steps_of(rng, shape, cuts, -0.22, 0.18) * values
    return jnp.clip(values, min=-most, max=most).astype(kind)


def setup_inputs(seed: int = 0) -> dict:
    splits = jax.random.split(jax.random.key(seed), 7)
    tokens = bell_draw(splits[0], (TOKENS, D), 1.0, 6.0, ((0, 16),))
    routes = draw_routes(jax.random.fold_in(splits[6], 71), 0)
    combine = jnp.clip(0.049804688 + 0.3486328 * jax.random.uniform(splits[2], (TOKENS, TOP), jnp.float32) ** steps_of(splits[2], (TOKENS, TOP), ((0, 16),), -0.2, 0.2), 0.049804688, 0.3984375).astype(jnp.bfloat16)
    gate_weight = bell_draw(splits[3], (EXPERTS * FF, D), D ** -0.5, 0.125, ((0, 1024),))
    up_weight = bell_draw(splits[4], (EXPERTS * FF, D), D ** -0.5, 0.125, ((0, 1024),))
    direction = bell_draw(splits[5], (EXPERTS * FF, D), 0.05, 0.29882812, ((0, 1024),))
    return dict(tokens=tokens, routes=routes, combine=combine, gate_weight=gate_weight, up_weight=up_weight, direction=direction)


def reference(tokens, routes, combine, gate_weight, up_weight, direction):
    block_count = TOKENS // COL_TOK
    slot_total = block_count * CAP
    expert_ids = jnp.arange(EXPERTS, dtype=jnp.int32)

    def per_expert(tangent_sum, expert_id):
        matches = routes == expert_id
        member = jnp.any(matches, axis=1).reshape(block_count, COL_TOK)
        weight_tok = jnp.sum(jnp.where(matches, combine.astype(jnp.float32), 0.0), axis=1)
        slot_rank = (jnp.cumsum(member.astype(jnp.int32), axis=1) - 1).astype(jnp.int32)
        slot_ids = jnp.arange(CAP, dtype=jnp.int32)
        picked_slots = member[:, None, :] & (slot_rank[:, None, :] == slot_ids[None, :, None])
        token_ids = jnp.arange(COL_TOK, dtype=jnp.int32)
        token_index = jnp.sum(jnp.where(picked_slots, token_ids[None, None, :], 0), axis=2).astype(jnp.int32)
        token_index = (token_index + jnp.arange(block_count, dtype=jnp.int32)[:, None] * COL_TOK).reshape(slot_total)
        filled = jnp.any(picked_slots, axis=2).reshape(slot_total)
        slot_rows = jnp.where(filled[:, None], tokens[token_index], jnp.zeros((), tokens.dtype))
        slot_weight = jnp.where(filled, weight_tok[token_index], 0.0)
        first_row = (expert_id * FF).astype(jnp.int32)
        expert_gate = lax.dynamic_slice_in_dim(gate_weight, first_row, FF, 0)
        expert_up = lax.dynamic_slice_in_dim(up_weight, first_row, FF, 0)
        expert_direction = lax.dynamic_slice_in_dim(direction, first_row, FF, 0)
        gate_value = jnp.dot(slot_rows, expert_gate.T, preferred_element_type=jnp.float32)
        up_value = jnp.dot(slot_rows, expert_up.T, preferred_element_type=jnp.float32)
        hidden = (jax.nn.silu(gate_value) * up_value).astype(jnp.bfloat16)
        slice_out = jnp.einsum("rsu,sud->rsd", hidden.reshape(slot_total, SPLIT, UNITS).astype(jnp.float32),
                               expert_direction.reshape(SPLIT, UNITS, D).astype(jnp.float32)).astype(jnp.bfloat16)
        contrib = jnp.sum(slice_out.astype(jnp.float32) * slot_weight[:, None, None], axis=1)
        contrib = jnp.where(filled[:, None], contrib, 0.0)
        tangent_sum = tangent_sum.at[token_index].add(contrib)
        return tangent_sum, (hidden, token_index, filled, slot_weight)

    start = jnp.zeros((TOKENS, D), jnp.float32)
    tangent_sum, stacked = lax.scan(per_expert, start, expert_ids)
    tangent_out = tangent_sum.astype(jnp.bfloat16)

    def curvature_of(pieces):
        hidden, token_index, filled, slot_weight = pieces
        picked = tangent_out[token_index].astype(jnp.float32)
        scaled = jnp.where(filled[:, None], picked * slot_weight[:, None], 0.0).astype(jnp.bfloat16)
        return jnp.dot(hidden.T, scaled, preferred_element_type=jnp.float32).astype(jnp.bfloat16)

    curvature = lax.map(curvature_of, stacked).reshape(EXPERTS * FF, D)
    return (tangent_out, curvature)
```

```python
import jax
import jax.numpy as jnp
from jax import lax
from jax.sharding import Mesh, PartitionSpec as P

TOP = 8
EXP_COL = 8
CORES = 2
LINE = 4


def contract_rows(left, right):
    return lax.dot_general(
        left, right, (((0,), (0,)), ((), ())), preferred_element_type=jnp.float32
    )


def shift_line(value, step):
    return lax.ppermute(value, "line", [(i, (i + step) % LINE) for i in range(LINE)])


def swap_cores(value):
    return lax.ppermute(value, "core", [(i, i ^ 1) for i in range(CORES)])


def swap_local(value, mask):
    return lax.ppermute(value, "local", [(i, i ^ mask) for i in range(EXP_COL)])


def shards(tokens, routes, combine, gate_weight, up_weight, direction):
    n_expert = lax.axis_size("expert")
    n_slice = LINE * CORES
    col_tok, width = tokens.shape
    unit_count = gate_weight.shape[0]
    cols = width // n_slice
    slot_count = 2 * col_tok * TOP // (EXP_COL * n_expert)
    rows = n_expert * slot_count
    local_index = lax.axis_index("local")
    line_index = lax.axis_index("line")
    core_index = lax.axis_index("core")

    def first_col(step, other):
        line = (line_index + step) & (LINE - 1)
        core = core_index ^ other
        return (line * CORES + core) * cols

    def columns(weight, step, other):
        return lax.dynamic_slice_in_dim(weight, first_col(step, other), cols, 1)

    with jax.named_scope("routing"):
        owner_ids = jnp.arange(n_expert, dtype=jnp.int32) * EXP_COL + local_index
        matches = routes[None, :, :] == owner_ids[:, None, None]
        member = jnp.any(matches, axis=2)
        weight_tok = jnp.sum(
            jnp.where(matches, combine[None, :, :].astype(jnp.float32), 0.0), axis=2
        )
        slot_rank = jnp.cumsum(member.astype(jnp.int32), axis=1) - 1
        slot_ids = jnp.arange(slot_count, dtype=jnp.int32)
        picked_slots = member[:, None, :] & (slot_rank[:, None, :] == slot_ids[None, :, None])
        select = picked_slots.astype(jnp.bfloat16).reshape(rows, col_tok)
        weighted = jnp.where(picked_slots, weight_tok[:, None, :], 0.0)
        slot_weight = jnp.sum(weighted, axis=2).reshape(rows, 1)
        spread = weighted.astype(jnp.bfloat16).reshape(rows, col_tok)

    def over_planes(slots):
        moved = lax.all_to_all(
            slots.reshape(n_expert, slot_count, cols), "expert", 0, 0, tiled=True
        )
        return moved.reshape(rows, cols)

    def gather_blocks(block):
        blocks = {(0, 0): block}
        for step in (2, 1, 3):
            blocks[(LINE - step, 0)] = shift_line(block, step)
        for step in (0, 1, 3, 2):
            blocks[(step, 1)] = swap_cores(blocks[(step, 0)])
        return blocks

    with jax.named_scope("dispatch"):
        own_cols = columns(tokens, 0, 0)
        outgoing = jnp.dot(select, own_cols, preferred_element_type=jnp.float32)
        row_blocks = gather_blocks(over_planes(outgoing.astype(jnp.bfloat16)))

    with jax.named_scope("experts"):
        both = jnp.concatenate([gate_weight, up_weight], axis=0)
        value = 0.0
        for (step, other), block in row_blocks.items():
            value += lax.dot_general(
                block,
                columns(both, step, other),
                (((1,), (1,)), ((), ())),
                preferred_element_type=jnp.float32,
            )
        hidden = jax.nn.silu(value[:, :unit_count]) * value[:, unit_count:]
        hidden = hidden.astype(jnp.bfloat16)

    with jax.named_scope("combine"):
        def slice_out(step, other):
            return jnp.dot(
                hidden, columns(direction, step, other), preferred_element_type=jnp.float32
            )

        steps = (2, 1, 3, 0)
        swapped = {
            step: swap_cores(slice_out(step, 1).astype(jnp.bfloat16)) for step in steps
        }
        pair_out = {
            step: (slice_out(step, 0) + swapped[step].astype(jnp.float32)).astype(jnp.bfloat16)
            for step in steps
        }
        expert_out = pair_out[0].astype(jnp.float32)
        for step in steps[:3]:
            expert_out += shift_line(pair_out[step], step).astype(jnp.float32)
        returned = over_planes(expert_out.astype(jnp.bfloat16))
        part = lax.optimization_barrier(contract_rows(spread, returned).astype(jnp.bfloat16))
        near = [swap_local(part, mask).astype(jnp.float32) for mask in (2, 4, 6)]
        half = (part.astype(jnp.float32) + near[0]) + (near[1] + near[2])
        half = lax.optimization_barrier(half.astype(jnp.bfloat16))
        total = half.astype(jnp.float32) + swap_local(half, 1).astype(jnp.float32)
        tangent_cols = total.astype(jnp.bfloat16)

    with jax.named_scope("tangent"):
        tangent_out = lax.all_gather(tangent_cols, ("line", "core"))
        tangent_out = tangent_out.transpose(1, 0, 2).reshape(col_tok, width)

    with jax.named_scope("curvature"):
        picked = jnp.dot(select, tangent_cols, preferred_element_type=jnp.float32)
        scaled = (picked * slot_weight).astype(jnp.bfloat16)
        curvature = jnp.zeros((unit_count, width), jnp.bfloat16)
        for (step, other), block in gather_blocks(over_planes(scaled)).items():
            curvature = lax.dynamic_update_slice_in_dim(
                curvature,
                contract_rows(hidden, block).astype(jnp.bfloat16),
                first_col(step, other),
                1,
            )
    return tangent_out, curvature


def solution(mesh):
    n_expert = mesh.shape["expert"]
    fine = Mesh(
        mesh.devices.reshape(n_expert, EXP_COL, LINE, CORES), ("expert", "local", "line", "core")
    )
    by_block = P("expert", None)
    by_device = P(("expert", "local", "line", "core"), None)
    return jax.shard_map(
        shards,
        mesh=fine,
        in_specs=(by_block, by_block, by_block, by_device, by_device, by_device),
        out_specs=(by_block, by_device),
        check_vma=False,
    )
```

```python
import jax
import jax.numpy as jnp
from jax import lax
from jax.sharding import Mesh, PartitionSpec as P

TOP = 8
EXP_COL = 8
CORES = 2
LINE = 4
STEPS = (2, 1, 3)


def contract_rows(left, right):
    return lax.dot_general(
        left, right, (((0,), (0,)), ((), ())), preferred_element_type=jnp.float32
    )


def shift_line(value, step):
    return lax.ppermute(value, "line", [(i, (i + step) % LINE) for i in range(LINE)])


def swap_cores(value):
    return lax.ppermute(value, "core", [(i, i ^ 1) for i in range(CORES)])


def swap_local(value, mask):
    return lax.ppermute(value, "local", [(i, i ^ mask) for i in range(EXP_COL)])


def gather_blocks(block):
    blocks = {(0, 0): block}
    for step in STEPS:
        blocks[(LINE - step, 0)] = shift_line(block, step)
    for step in (0, 1, 3, 2):
        blocks[(step, 1)] = swap_cores(blocks[(step, 0)])
    return blocks


def exchange_blocks(piece):
    steps = (*STEPS, 0)
    swapped = swap_cores(jnp.stack([piece(step, 1) for step in steps]))
    pairs = {step: jnp.stack([piece(step, 0), swapped[i]]) for i, step in enumerate(steps)}
    blocks = {}
    for step in STEPS:
        arrived = shift_line(pairs[step], step)
        blocks[(LINE - step, 0)], blocks[(LINE - step, 1)] = arrived[0], arrived[1]
    blocks[(0, 0)], blocks[(0, 1)] = pairs[0][0], pairs[0][1]
    return blocks


def shards(tokens, routes, combine, gate_weight, up_weight, direction):
    n_expert = lax.axis_size("expert")
    col_tok, width = tokens.shape
    unit_count = gate_weight.shape[0]
    cols = width // (LINE * CORES)
    slot_count = 2 * col_tok * TOP // (EXP_COL * n_expert)
    rows = n_expert * slot_count
    local_index = lax.axis_index("local")
    line_index = lax.axis_index("line")
    core_index = lax.axis_index("core")

    def first_col(step, other):
        line = (line_index + step) & (LINE - 1)
        return (line * CORES + (core_index ^ other)) * cols

    def columns(weight, step, other):
        return lax.dynamic_slice_in_dim(weight, first_col(step, other), cols, 1)

    def assemble(blocks, height):
        whole = jnp.zeros((height, width), jnp.bfloat16)
        for (step, other), block in blocks.items():
            whole = lax.dynamic_update_slice_in_dim(whole, block, first_col(step, other), 1)
        return whole

    with jax.named_scope("routing"):
        owner_ids = jnp.arange(n_expert, dtype=jnp.int32) * EXP_COL + local_index
        matches = routes[None, :, :] == owner_ids[:, None, None]
        member = jnp.any(matches, axis=2)
        weight_tok = jnp.sum(
            jnp.where(matches, combine[None, :, :].astype(jnp.float32), 0.0), axis=2
        )
        slot_rank = jnp.cumsum(member.astype(jnp.int32), axis=1) - 1
        slot_ids = jnp.arange(slot_count, dtype=jnp.int32)
        picked_slots = member[:, None, :] & (slot_rank[:, None, :] == slot_ids[None, :, None])
        select = picked_slots.astype(jnp.bfloat16).reshape(rows, col_tok)
        weighted = jnp.where(picked_slots, weight_tok[:, None, :], 0.0)
        slot_weight = jnp.sum(weighted, axis=2).reshape(rows, 1)
        spread = weighted.astype(jnp.bfloat16).reshape(rows, col_tok)

    def over_planes(slots):
        moved = lax.all_to_all(
            slots.reshape(n_expert, slot_count, cols), "expert", 0, 0, tiled=True
        )
        return moved.reshape(rows, cols)

    with jax.named_scope("dispatch"):
        outgoing = jnp.dot(select, columns(tokens, 0, 0), preferred_element_type=jnp.float32)
        arrived = over_planes(outgoing.astype(jnp.bfloat16))

    with jax.named_scope("direction"):
        direction_blocks = exchange_blocks(lambda step, other: columns(direction, step, other))

    with jax.named_scope("experts"):
        both = jnp.concatenate([gate_weight, up_weight], axis=0)
        value = 0.0
        for (step, other), block in gather_blocks(arrived).items():
            value += lax.dot_general(
                columns(both, step, other),
                block,
                (((1,), (1,)), ((), ())),
                preferred_element_type=jnp.float32,
            )
        hidden = (jax.nn.silu(value[:unit_count]) * value[unit_count:]).astype(jnp.bfloat16)
        hidden_blocks = gather_blocks(hidden)

    with jax.named_scope("combine"):
        expert_out = 0.0
        for key, block in hidden_blocks.items():
            expert_out += contract_rows(block, direction_blocks[key])
        returned = over_planes(expert_out.astype(jnp.bfloat16))
        part = lax.optimization_barrier(contract_rows(spread, returned).astype(jnp.bfloat16))
        near = [swap_local(part, mask).astype(jnp.float32) for mask in (4, 2, 6)]
        half = (part.astype(jnp.float32) + near[1]) + (near[0] + near[2])
        half = lax.optimization_barrier(half.astype(jnp.bfloat16))
        total = half.astype(jnp.float32) + swap_local(half, 1).astype(jnp.float32)
        tangent_cols = total.astype(jnp.bfloat16)

    with jax.named_scope("curvature"):
        picked = jnp.dot(select, tangent_cols, preferred_element_type=jnp.float32)
        scaled = over_planes((picked * slot_weight).astype(jnp.bfloat16))

    with jax.named_scope("tangent"):
        tangent_out = assemble(gather_blocks(tangent_cols), col_tok)

    with jax.named_scope("curvature"):
        def product(step, other):
            value = jnp.dot(
                hidden_blocks[(step, other)], scaled, preferred_element_type=jnp.float32
            )
            return value.astype(jnp.bfloat16)

        curvature = assemble(exchange_blocks(product), unit_count)
    return tangent_out, curvature


def solution(mesh):
    n_expert = mesh.shape["expert"]
    fine = Mesh(
        mesh.devices.reshape(n_expert, EXP_COL, LINE, CORES), ("expert", "local", "line", "core")
    )
    by_block = P("expert", None)
    by_device = P(("expert", "local", "line", "core"), None)
    return jax.shard_map(
        shards,
        mesh=fine,
        in_specs=(by_block, by_block, by_block, by_device, by_device, by_device),
        out_specs=(by_block, by_device),
        check_vma=False,
    )
```

```python
import jax
import jax.numpy as jnp
from jax import lax
from jax.sharding import Mesh, PartitionSpec as P

TOP = 8
EXP_COL = 8
CORES = 2
LINE = 4
STEPS = (2, 1, 3)


def contract_rows(left, right):
    return lax.dot_general(
        left, right, (((0,), (0,)), ((), ())), preferred_element_type=jnp.float32
    )


def shift_line(value, step):
    return lax.ppermute(value, "line", [(i, (i + step) % LINE) for i in range(LINE)])


def swap_cores(value):
    return lax.ppermute(value, "core", [(i, i ^ 1) for i in range(CORES)])


def swap_local(value, mask):
    return lax.ppermute(value, "local", [(i, i ^ mask) for i in range(EXP_COL)])


def gather_blocks(block):
    blocks = {(0, 0): block}
    for step in STEPS:
        blocks[(LINE - step, 0)] = shift_line(block, step)
    for step in (0, 1, 3, 2):
        blocks[(step, 1)] = swap_cores(blocks[(step, 0)])
    return blocks


def pair_shift(pairs):
    blocks = {(0, 0): pairs[0][0], (0, 1): pairs[0][1]}
    for step in STEPS:
        arrived = shift_line(jnp.stack(pairs[step]), step)
        blocks[(LINE - step, 0)], blocks[(LINE - step, 1)] = arrived[0], arrived[1]
    return blocks


def shards(tokens, routes, combine, gate_weight, up_weight, direction):
    n_expert = lax.axis_size("expert")
    col_tok, width = tokens.shape
    unit_count = gate_weight.shape[0]
    cols = width // (LINE * CORES)
    slot_count = 2 * col_tok * TOP // (EXP_COL * n_expert)
    rows = n_expert * slot_count
    local_index = lax.axis_index("local")
    line_index = lax.axis_index("line")
    core_index = lax.axis_index("core")

    def first_col(step, other):
        line = (line_index + step) & (LINE - 1)
        return (line * CORES + (core_index ^ other)) * cols

    def columns(weight, step, other):
        return lax.dynamic_slice_in_dim(weight, first_col(step, other), cols, 1)

    def assemble(blocks, height):
        whole = jnp.zeros((height, width), jnp.bfloat16)
        for (step, other), block in blocks.items():
            whole = lax.dynamic_update_slice_in_dim(whole, block, first_col(step, other), 1)
        return whole

    with jax.named_scope("routing"):
        owner_ids = jnp.arange(n_expert, dtype=jnp.int32) * EXP_COL + local_index
        matches = routes[None, :, :] == owner_ids[:, None, None]
        member = jnp.any(matches, axis=2)
        weight_tok = jnp.sum(
            jnp.where(matches, combine[None, :, :].astype(jnp.float32), 0.0), axis=2
        )
        slot_rank = jnp.cumsum(member.astype(jnp.int32), axis=1) - 1
        slot_ids = jnp.arange(slot_count, dtype=jnp.int32)
        picked_slots = member[:, None, :] & (slot_rank[:, None, :] == slot_ids[None, :, None])
        select = picked_slots.astype(jnp.bfloat16).reshape(rows, col_tok)
        weighted = jnp.where(picked_slots, weight_tok[:, None, :], 0.0)
        slot_weight = jnp.sum(weighted, axis=2).reshape(rows, 1)
        spread = weighted.astype(jnp.bfloat16).reshape(rows, col_tok)

    def over_planes(slots):
        moved = lax.all_to_all(
            slots.reshape(n_expert, slot_count, cols), "expert", 0, 0, tiled=True
        )
        return moved.reshape(rows, cols)

    with jax.named_scope("direction"):
        swapped = swap_cores(jnp.stack([columns(direction, step, 1) for step in range(LINE)]))

    with jax.named_scope("dispatch"):
        outgoing = jnp.dot(select, columns(tokens, 0, 0), preferred_element_type=jnp.float32)
        outgoing, swapped = lax.optimization_barrier((outgoing.astype(jnp.bfloat16), swapped))
        arrived = over_planes(outgoing)

    with jax.named_scope("direction"):
        direction_blocks = pair_shift(
            [(columns(direction, step, 0), swapped[step]) for step in range(LINE)]
        )
        arrived, direction_blocks = lax.optimization_barrier((arrived, direction_blocks))

    with jax.named_scope("experts"):
        both = jnp.concatenate([gate_weight, up_weight], axis=0)
        value = 0.0
        for (step, other), block in gather_blocks(arrived).items():
            value += lax.dot_general(
                columns(both, step, other),
                block,
                (((1,), (1,)), ((), ())),
                preferred_element_type=jnp.float32,
            )
        hidden = (jax.nn.silu(value[:unit_count]) * value[unit_count:]).astype(jnp.bfloat16)
        hidden_blocks = gather_blocks(hidden)

    with jax.named_scope("combine"):
        expert_out = 0.0
        for key, block in hidden_blocks.items():
            expert_out += contract_rows(block, direction_blocks[key])
        returned = over_planes(expert_out.astype(jnp.bfloat16))
        part = contract_rows(spread, returned).astype(jnp.bfloat16)
        first, second = lax.optimization_barrier((part[: col_tok // 2], part[col_tok // 2 :]))

        def add_half(value):
            return value.astype(jnp.float32) + swap_local(value, 1).astype(jnp.float32)

        def add_x(value):
            near, far, last = (swap_local(value, mask).astype(jnp.float32) for mask in (2, 4, 6))
            return (value.astype(jnp.float32) + near) + (far + last)

        second, first = lax.optimization_barrier(
            (add_half(second).astype(jnp.bfloat16), add_x(first).astype(jnp.bfloat16))
        )
        tangent_cols = jnp.concatenate([add_half(first), add_x(second)]).astype(jnp.bfloat16)

    with jax.named_scope("curvature"):
        picked = jnp.dot(select, tangent_cols, preferred_element_type=jnp.float32)
        scaled = over_planes((picked * slot_weight).astype(jnp.bfloat16))

    with jax.named_scope("tangent"):
        tangent_out = assemble(gather_blocks(tangent_cols), col_tok)

    with jax.named_scope("curvature"):
        def product(block):
            value = jnp.dot(block, scaled, preferred_element_type=jnp.float32)
            return value.astype(jnp.bfloat16)

        other_units = jnp.concatenate([hidden_blocks[(step, 1)] for step in range(LINE)])
        crossed = swap_cores(product(other_units)).reshape(LINE, unit_count, cols)
        finished = {}
        for step in STEPS:
            finished[(LINE - step, 0)] = shift_line(product(hidden_blocks[(step, 0)]), step)
        for step in STEPS:
            finished[(LINE - step, 1)] = shift_line(crossed[step], step)
        finished[(0, 0)], finished[(0, 1)] = product(hidden_blocks[(0, 0)]), crossed[0]
        curvature = assemble(finished, unit_count)
    return tangent_out, curvature


def solution(mesh):
    n_expert = mesh.shape["expert"]
    fine = Mesh(
        mesh.devices.reshape(n_expert, EXP_COL, LINE, CORES), ("expert", "local", "line", "core")
    )
    by_block = P("expert", None)
    by_device = P(("expert", "local", "line", "core"), None)
    return jax.shard_map(
        shards,
        mesh=fine,
        in_specs=(by_block, by_block, by_block, by_device, by_device, by_device),
        out_specs=(by_block, by_device),
        check_vma=False,
    )
```

```python
import jax
import jax.numpy as jnp
from jax import lax
from jax.sharding import Mesh, PartitionSpec as P

TOP = 8
EXP_COL = 8
CORES = 2
LINE = 4
HALVES = 2
STEPS = (2, 1, 3)


def contract_rows(left, right):
    return lax.dot_general(
        left, right, (((0,), (0,)), ((), ())), preferred_element_type=jnp.float32
    )


def shift_line(value, step):
    return lax.ppermute(value, "line", [(i, (i + step) % LINE) for i in range(LINE)])


def swap_cores(value):
    return lax.ppermute(value, "core", [(i, i ^ 1) for i in range(CORES)])


def swap_halves(value):
    return lax.ppermute(value, "half", [(i, i ^ 1) for i in range(HALVES)])


def shards(tokens, routes, combine, gate_weight, up_weight, direction):
    n_expert = lax.axis_size("expert")
    n_slice = LINE * CORES
    col_tok, width = tokens.shape
    unit_count = gate_weight.shape[0]
    cols = width // n_slice
    slot_count = 2 * col_tok * TOP // (EXP_COL * n_expert)
    rows = n_expert * slot_count
    local_index = lax.axis_index(("x", "half"))
    line_index = lax.axis_index("line")
    core_index = lax.axis_index("core")

    def first_col(step, other):
        line = (line_index + step) & (LINE - 1)
        core = core_index ^ other
        return (line * CORES + core) * cols

    def columns(weight, step, other):
        return lax.dynamic_slice_in_dim(weight, first_col(step, other), cols, 1)

    with jax.named_scope("routing"):
        owner_ids = jnp.arange(n_expert, dtype=jnp.int32) * EXP_COL + local_index
        matches = routes[None, :, :] == owner_ids[:, None, None]
        member = jnp.any(matches, axis=2)
        weight_tok = jnp.sum(
            jnp.where(matches, combine[None, :, :].astype(jnp.float32), 0.0), axis=2
        )
        slot_rank = jnp.cumsum(member.astype(jnp.int32), axis=1) - 1
        slot_ids = jnp.arange(slot_count, dtype=jnp.int32)
        picked_slots = member[:, None, :] & (slot_rank[:, None, :] == slot_ids[None, :, None])
        select = picked_slots.astype(jnp.bfloat16).reshape(rows, col_tok)
        weighted = jnp.where(picked_slots, weight_tok[:, None, :], 0.0)
        slot_weight = jnp.sum(weighted, axis=2).reshape(rows, 1)
        spread = weighted.astype(jnp.bfloat16).reshape(rows, col_tok)

    def over_planes(slots):
        moved = lax.all_to_all(
            slots.reshape(n_expert, slot_count, cols), "expert", 0, 0, tiled=True
        )
        return moved.reshape(rows, cols)

    def gather_blocks(block):
        blocks = {(0, 0): block}
        for step in STEPS:
            blocks[(LINE - step, 0)] = shift_line(block, step)
        for step in (0, 1, 3, 2):
            blocks[(step, 1)] = swap_cores(blocks[(step, 0)])
        return blocks

    with jax.named_scope("dispatch"):
        own_cols = columns(tokens, 0, 0)
        outgoing = jnp.dot(select, own_cols, preferred_element_type=jnp.float32)
        row_blocks = gather_blocks(over_planes(outgoing.astype(jnp.bfloat16)))

    with jax.named_scope("experts"):
        both = jnp.concatenate([gate_weight, up_weight], axis=0)
        value = 0.0
        for (step, other), block in row_blocks.items():
            value += lax.dot_general(
                block,
                columns(both, step, other),
                (((1,), (1,)), ((), ())),
                preferred_element_type=jnp.float32,
            )
        hidden = jax.nn.silu(value[:, :unit_count]) * value[:, unit_count:]
        hidden = hidden.astype(jnp.bfloat16)

    with jax.named_scope("combine"):
        other_cols = jnp.concatenate([columns(direction, step, 1) for step in range(LINE)], axis=1)
        crossed = swap_cores(
            jnp.dot(hidden, other_cols, preferred_element_type=jnp.float32).astype(jnp.bfloat16)
        )

        def pair_out(step):
            own = jnp.dot(
                hidden, columns(direction, step, 0), preferred_element_type=jnp.float32
            )
            other = crossed[:, step * cols : (step + 1) * cols].astype(jnp.float32)
            return (own + other).astype(jnp.bfloat16)

        arrived = [shift_line(pair_out(step), step).astype(jnp.float32) for step in STEPS]
        expert_out = pair_out(0).astype(jnp.float32) + arrived[0] + arrived[1] + arrived[2]
        returned = over_planes(expert_out.astype(jnp.bfloat16))
        part = contract_rows(spread, returned).astype(jnp.bfloat16)
        parts = lax.all_to_all(
            jnp.broadcast_to(part, (EXP_COL // HALVES, col_tok, cols)), "x", 0, 0, tiled=True
        )
        half = jnp.sum(parts.astype(jnp.float32), axis=0).astype(jnp.bfloat16)
        half = lax.optimization_barrier(half)
        total = half.astype(jnp.float32) + swap_halves(half).astype(jnp.float32)
        tangent_cols = total.astype(jnp.bfloat16)

    with jax.named_scope("curvature"):
        picked = jnp.dot(select, tangent_cols, preferred_element_type=jnp.float32)
        scaled = (picked * slot_weight).astype(jnp.bfloat16)
        scaled, tangent_late = lax.optimization_barrier((scaled, tangent_cols))
        moved = over_planes(scaled)

    with jax.named_scope("tangent"):
        tangent_out = jnp.zeros((col_tok, width), jnp.bfloat16)
        for (step, other), block in gather_blocks(tangent_late).items():
            tangent_out = lax.dynamic_update_slice_in_dim(
                tangent_out, block, first_col(step, other), 1
            )

    with jax.named_scope("curvature"):
        curvature = jnp.zeros((unit_count, width), jnp.bfloat16)
        for (step, other), block in gather_blocks(moved).items():
            curvature = lax.dynamic_update_slice_in_dim(
                curvature,
                contract_rows(hidden, block).astype(jnp.bfloat16),
                first_col(step, other),
                1,
            )
    return tangent_out, curvature


def solution(mesh):
    n_expert = mesh.shape["expert"]
    fine = Mesh(
        mesh.devices.reshape(n_expert, EXP_COL // HALVES, HALVES, LINE, CORES),
        ("expert", "x", "half", "line", "core"),
    )
    by_block = P("expert", None)
    by_device = P(("expert", "x", "half", "line", "core"), None)
    return jax.shard_map(
        shards,
        mesh=fine,
        in_specs=(by_block, by_block, by_block, by_device, by_device, by_device),
        out_specs=(by_block, by_device),
        check_vma=False,
    )
```

```python
import jax
import jax.numpy as jnp
from jax import lax
from jax.sharding import Mesh, PartitionSpec as P

TOP = 8
EXP_COL = 8
CORES = 2
LINE = 4
HALVES = 2
MASKS = (1, 2, 3)


def contract_rows(left, right):
    return lax.dot_general(
        left, right, (((0,), (0,)), ((), ())), preferred_element_type=jnp.float32
    )


def swap_line(value, mask):
    return lax.ppermute(value, "line", [(i, i ^ mask) for i in range(LINE)])


def swap_cores(value):
    return lax.ppermute(value, "core", [(i, i ^ 1) for i in range(CORES)])


def swap_halves(value):
    return lax.ppermute(value, "half", [(i, i ^ 1) for i in range(HALVES)])


def shards(tokens, routes, combine, gate_weight, up_weight, direction):
    n_expert = lax.axis_size("expert")
    n_slice = LINE * CORES
    col_tok, width = tokens.shape
    unit_count = gate_weight.shape[0]
    cols = width // n_slice
    slot_count = 2 * col_tok * TOP // (EXP_COL * n_expert)
    rows = n_expert * slot_count
    local_index = lax.axis_index(("x", "half"))
    line_index = lax.axis_index("line")
    core_index = lax.axis_index("core")

    def first_col(mask, other):
        return ((line_index ^ mask) * CORES + (core_index ^ other)) * cols

    def columns(weight, mask, other):
        return lax.dynamic_slice_in_dim(weight, first_col(mask, other), cols, 1)

    with jax.named_scope("routing"):
        owner_ids = jnp.arange(n_expert, dtype=jnp.int32) * EXP_COL + local_index
        matches = routes[None, :, :] == owner_ids[:, None, None]
        member = jnp.any(matches, axis=2)
        weight_tok = jnp.sum(
            jnp.where(matches, combine[None, :, :].astype(jnp.float32), 0.0), axis=2
        )
        slot_rank = jnp.cumsum(member.astype(jnp.int32), axis=1) - 1
        slot_ids = jnp.arange(slot_count, dtype=jnp.int32)
        picked_slots = member[:, None, :] & (slot_rank[:, None, :] == slot_ids[None, :, None])
        select = picked_slots.astype(jnp.bfloat16).reshape(rows, col_tok)
        weighted = jnp.where(picked_slots, weight_tok[:, None, :], 0.0)
        slot_weight = jnp.sum(weighted, axis=2).reshape(rows, 1)
        spread = weighted.astype(jnp.bfloat16).reshape(rows, col_tok)

    def over_planes(slots):
        moved = lax.all_to_all(
            slots.reshape(n_expert, slot_count, cols), "expert", 0, 0, tiled=True
        )
        return moved.reshape(rows, cols)

    def with_cores(pieces):
        crossed = swap_cores(jnp.concatenate(pieces)).reshape(LINE, *pieces[0].shape)
        return {
            (mask, other): (pieces[mask], crossed[mask])[other]
            for other in range(CORES)
            for mask in range(LINE)
        }

    def gather_line(block):
        return [block, *(swap_line(block, mask) for mask in MASKS)]

    with jax.named_scope("dispatch"):
        own_cols = columns(tokens, 0, 0)
        outgoing = jnp.dot(select, own_cols, preferred_element_type=jnp.float32)
        arrived = over_planes(outgoing.astype(jnp.bfloat16))
        other_cols = jnp.concatenate([columns(direction, mask, 1) for mask in range(LINE)], axis=1)
        both = jnp.concatenate([gate_weight, up_weight], axis=0)
        arrived, other_cols, both = lax.optimization_barrier((arrived, other_cols, both))
        row_blocks = with_cores(gather_line(arrived))

    with jax.named_scope("experts"):
        value = 0.0
        for (mask, other), block in row_blocks.items():
            value += lax.dot_general(
                block,
                columns(both, mask, other),
                (((1,), (1,)), ((), ())),
                preferred_element_type=jnp.float32,
            )
        hidden = jax.nn.silu(value[:, :unit_count]) * value[:, unit_count:]
        hidden = hidden.astype(jnp.bfloat16)

    with jax.named_scope("combine"):
        crossed = swap_cores(
            jnp.dot(hidden, other_cols, preferred_element_type=jnp.float32).astype(jnp.bfloat16)
        )

        def pair_out(mask):
            own = jnp.dot(
                hidden, columns(direction, mask, 0), preferred_element_type=jnp.float32
            )
            other = crossed[:, mask * cols : (mask + 1) * cols].astype(jnp.float32)
            return (own + other).astype(jnp.bfloat16)

        arrived = [swap_line(pair_out(mask), mask).astype(jnp.float32) for mask in MASKS]
        expert_out = pair_out(0).astype(jnp.float32) + arrived[0] + arrived[1] + arrived[2]
        returned = over_planes(expert_out.astype(jnp.bfloat16))
        part = contract_rows(spread, returned).astype(jnp.bfloat16)
        parts = lax.all_to_all(
            jnp.broadcast_to(part, (EXP_COL // HALVES, col_tok, cols)), "x", 0, 0, tiled=True
        )
        half = jnp.sum(parts.astype(jnp.float32), axis=0).astype(jnp.bfloat16)
        half = lax.optimization_barrier(half)
        total = half.astype(jnp.float32) + swap_halves(half).astype(jnp.float32)
        tangent_cols = total.astype(jnp.bfloat16)

    with jax.named_scope("curvature"):
        picked = jnp.dot(select, tangent_cols, preferred_element_type=jnp.float32)
        scaled = (picked * slot_weight).astype(jnp.bfloat16)
        scaled, tangent_late = lax.optimization_barrier((scaled, tangent_cols))
        moved = over_planes(scaled)

    with jax.named_scope("tangent"):
        pieces = gather_line(tangent_late)
        moved, *pieces = lax.optimization_barrier((moved, *pieces))

    with jax.named_scope("curvature"):
        scaled_blocks = with_cores(gather_line(moved))
        curvature = jnp.zeros((unit_count, width), jnp.bfloat16)
        for (mask, other), block in scaled_blocks.items():
            curvature = lax.dynamic_update_slice_in_dim(
                curvature,
                contract_rows(hidden, block).astype(jnp.bfloat16),
                first_col(mask, other),
                1,
            )

    with jax.named_scope("tangent"):
        tangent_out = jnp.zeros((col_tok, width), jnp.bfloat16)
        for (mask, other), block in with_cores(pieces).items():
            tangent_out = lax.dynamic_update_slice_in_dim(
                tangent_out, block, first_col(mask, other), 1
            )
    return tangent_out, curvature


def solution(mesh):
    n_expert = mesh.shape["expert"]
    fine = Mesh(
        mesh.devices.reshape(n_expert, EXP_COL // HALVES, HALVES, LINE, CORES),
        ("expert", "x", "half", "line", "core"),
    )
    by_block = P("expert", None)
    by_device = P(("expert", "x", "half", "line", "core"), None)
    return jax.shard_map(
        shards,
        mesh=fine,
        in_specs=(by_block, by_block, by_block, by_device, by_device, by_device),
        out_specs=(by_block, by_device),
        check_vma=False,
    )
```

```python
import jax
import jax.numpy as jnp
from jax import lax
from jax.sharding import Mesh, PartitionSpec as P

TOP = 8
EXP_COL = 8
CORES = 2
LINE = 4
HALVES = 2
MASKS = (1, 2, 3)


def contract_rows(left, right):
    return lax.dot_general(
        left, right, (((0,), (0,)), ((), ())), preferred_element_type=jnp.float32
    )


def swap_line(value, mask):
    return lax.ppermute(value, "line", [(i, i ^ mask) for i in range(LINE)])


def swap_cores(value):
    return lax.ppermute(value, "core", [(i, i ^ 1) for i in range(CORES)])


def swap_halves(value):
    return lax.ppermute(value, "half", [(i, i ^ 1) for i in range(HALVES)])


def shards(tokens, routes, combine, gate_weight, up_weight, direction):
    n_expert = lax.axis_size("expert")
    n_slice = LINE * CORES
    col_tok, width = tokens.shape
    unit_count = gate_weight.shape[0]
    cols = width // n_slice
    slot_count = 2 * col_tok * TOP // (EXP_COL * n_expert)
    rows = n_expert * slot_count
    local_index = lax.axis_index(("x", "half"))
    line_index = lax.axis_index("line")
    core_index = lax.axis_index("core")

    def first_col(mask, other):
        return ((line_index ^ mask) * CORES + (core_index ^ other)) * cols

    def columns(weight, mask, other):
        return lax.dynamic_slice_in_dim(weight, first_col(mask, other), cols, 1)

    with jax.named_scope("routing"):
        owner_ids = jnp.arange(n_expert, dtype=jnp.int32) * EXP_COL + local_index
        matches = routes[None, :, :] == owner_ids[:, None, None]
        member = jnp.any(matches, axis=2)
        weight_tok = jnp.sum(
            jnp.where(matches, combine[None, :, :].astype(jnp.float32), 0.0), axis=2
        )
        slot_rank = jnp.cumsum(member.astype(jnp.int32), axis=1) - 1
        slot_ids = jnp.arange(slot_count, dtype=jnp.int32)
        picked_slots = member[:, None, :] & (slot_rank[:, None, :] == slot_ids[None, :, None])
        select = picked_slots.astype(jnp.bfloat16).reshape(rows, col_tok)
        weighted = jnp.where(picked_slots, weight_tok[:, None, :], 0.0)
        slot_weight = jnp.sum(weighted, axis=2).reshape(rows, 1)
        spread = weighted.astype(jnp.bfloat16).reshape(rows, col_tok)

    def over_planes(slots):
        moved = lax.all_to_all(
            slots.reshape(n_expert, slot_count, cols), "expert", 0, 0, tiled=True
        )
        return moved.reshape(rows, cols)

    def swap_in_two(pieces):
        half = LINE // 2
        crossed = []
        for group in (pieces[:half], pieces[half:]):
            arrived = swap_cores(jnp.concatenate(group))
            crossed += list(arrived.reshape(half, *group[0].shape))
        return crossed

    def place(whole, pieces, other):
        for mask in reversed(range(LINE)):
            whole = lax.dynamic_update_slice_in_dim(whole, pieces[mask], first_col(mask, other), 1)
        return whole

    def gather_line(block):
        return [block, *(swap_line(block, mask) for mask in MASKS)]

    with jax.named_scope("dispatch"):
        own_cols = columns(tokens, 0, 0)
        outgoing = jnp.dot(select, own_cols, preferred_element_type=jnp.float32)
        arrived = over_planes(outgoing.astype(jnp.bfloat16))
        direction_other = swap_cores(
            jnp.concatenate([columns(direction, mask, 1) for mask in range(LINE)], axis=1)
        )
        both = jnp.concatenate([gate_weight, up_weight], axis=0)
        arrived, direction_other, both = lax.optimization_barrier((arrived, direction_other, both))
        near_blocks = gather_line(arrived)
        row_blocks = {(mask, 0): block for mask, block in enumerate(near_blocks)}
        for mask, block in enumerate(swap_in_two(near_blocks)):
            row_blocks[(mask, 1)] = block

    with jax.named_scope("experts"):
        value = 0.0
        for (mask, other), block in row_blocks.items():
            value += lax.dot_general(
                block,
                columns(both, mask, other),
                (((1,), (1,)), ((), ())),
                preferred_element_type=jnp.float32,
            )
        hidden = jax.nn.silu(value[:, :unit_count]) * value[:, unit_count:]
        hidden = hidden.astype(jnp.bfloat16)
        hidden_other = swap_cores(hidden)

    with jax.named_scope("combine"):
        def pair_out(mask):
            own = jnp.dot(
                hidden, columns(direction, mask, 0), preferred_element_type=jnp.float32
            )
            other = jnp.dot(
                hidden_other,
                direction_other[:, mask * cols : (mask + 1) * cols],
                preferred_element_type=jnp.float32,
            )
            return (own + other).astype(jnp.bfloat16)

        arrived = [swap_line(pair_out(mask), mask).astype(jnp.float32) for mask in MASKS]
        expert_out = pair_out(0).astype(jnp.float32) + arrived[0] + arrived[1] + arrived[2]
        returned = over_planes(expert_out.astype(jnp.bfloat16))
        part = contract_rows(spread, returned).astype(jnp.bfloat16)
        parts = lax.all_to_all(
            jnp.broadcast_to(part, (EXP_COL // HALVES, col_tok, cols)), "x", 0, 0, tiled=True
        )
        half = jnp.sum(parts.astype(jnp.float32), axis=0).astype(jnp.bfloat16)
        half = lax.optimization_barrier(half)
        total = half.astype(jnp.float32) + swap_halves(half).astype(jnp.float32)
        tangent_cols = total.astype(jnp.bfloat16)

    with jax.named_scope("curvature"):
        picked = jnp.dot(select, tangent_cols, preferred_element_type=jnp.float32)
        scaled = (picked * slot_weight).astype(jnp.bfloat16)
        scaled, tangent_late = lax.optimization_barrier((scaled, tangent_cols))
        moved = over_planes(scaled)

    with jax.named_scope("tangent"):
        pieces = gather_line(tangent_late)
        moved, *pieces = lax.optimization_barrier((moved, *pieces))

    with jax.named_scope("curvature"):
        scaled_blocks = gather_line(moved)

        def products(units):
            return [contract_rows(units, block).astype(jnp.bfloat16) for block in scaled_blocks]

        curvature = jnp.zeros((unit_count, width), jnp.bfloat16)
        curvature = place(curvature, products(hidden), 0)
        curvature = place(curvature, swap_in_two(products(hidden_other)), 1)

    with jax.named_scope("tangent"):
        tangent_out = place(jnp.zeros((col_tok, width), jnp.bfloat16), pieces, 0)
        crossed = swap_cores(jnp.concatenate(pieces)).reshape(LINE, col_tok, cols)
        tangent_out = place(tangent_out, list(crossed), 1)
    return tangent_out, curvature


def solution(mesh):
    n_expert = mesh.shape["expert"]
    fine = Mesh(
        mesh.devices.reshape(n_expert, EXP_COL // HALVES, HALVES, LINE, CORES),
        ("expert", "x", "half", "line", "core"),
    )
    by_block = P("expert", None)
    by_device = P(("expert", "x", "half", "line", "core"), None)
    return jax.shard_map(
        shards,
        mesh=fine,
        in_specs=(by_block, by_block, by_block, by_device, by_device, by_device),
        out_specs=(by_block, by_device),
        check_vma=False,
    )
```

```python
import jax
import jax.numpy as jnp
from jax import lax
from jax.sharding import Mesh, PartitionSpec as P

TOP = 8
EXP_COL = 8
CORES = 2
LINE = 4
HALVES = 2


def contract_rows(left, right):
    return lax.dot_general(
        left, right, (((0,), (0,)), ((), ())), preferred_element_type=jnp.float32
    )


def send_line(value, pairs):
    return lax.ppermute(value, "line", pairs)


PAIRS = [(0, 1), (1, 0), (2, 3), (3, 2)]
INNER = [(1, 2), (2, 1)]
OUTWARD = [(1, 0), (2, 3)]
INWARD = [(0, 1), (3, 2)]
FAR_OUT = [(2, 0), (1, 3)]
FAR_IN = [(0, 2), (3, 1)]


def gather_line(block):
    paired = send_line(block, PAIRS)
    inner = send_line(block, INNER)
    second = inner + send_line(inner, OUTWARD)
    third = send_line(paired, INNER) + send_line(paired, FAR_OUT)
    return [block, paired, second, third]


def reduce_line(pieces):
    def send(value, pairs):
        return send_line(value.astype(jnp.bfloat16), pairs)

    far = send(pieces[3], FAR_IN)
    inner, near = send(pieces[2], INNER), send(pieces[2], INWARD)
    far, inner, near = lax.optimization_barrier((far, inner, near))
    paired, crossed = send(pieces[1] + far + inner, PAIRS), send(pieces[3] + near, INNER)
    return pieces[0] + paired + crossed


def gather_ring(block):
    ring = HALVES * LINE
    return [
        block,
        *(
            lax.ppermute(block, ("half", "line"), [(i, (i + step) % ring) for i in range(ring)])
            for step in (1, ring - 1, 2)
        ),
    ]


def swap_cores(value):
    return lax.ppermute(value, "core", [(i, i ^ 1) for i in range(CORES)])


def swap_halves(value):
    return lax.ppermute(value, "half", [(i, i ^ 1) for i in range(HALVES)])


def shards(tokens, routes, combine, gate_weight, up_weight, direction):
    n_expert = lax.axis_size("expert")
    n_slice = LINE * CORES
    col_tok, width = tokens.shape
    unit_count = gate_weight.shape[0]
    cols = width // n_slice
    slot_count = 2 * col_tok * TOP // (EXP_COL * n_expert)
    rows = n_expert * slot_count
    local_index = lax.axis_index(("x", "half"))
    line_index = lax.axis_index("line")
    core_index = lax.axis_index("core")

    is_inner = ((line_index == 1) | (line_index == 2)).astype(jnp.int32)
    gathered = [line_index ^ mask for mask in (0, 1, 2 + is_inner, 3 - is_inner)]

    def first_col(line, other):
        return ((line & (LINE - 1)) * CORES + (core_index ^ other)) * cols

    def columns(weight, line, other):
        return lax.dynamic_slice_in_dim(weight, first_col(line, other), cols, 1)

    with jax.named_scope("routing"):
        owner_ids = jnp.arange(n_expert, dtype=jnp.int32) * EXP_COL + local_index
        matches = routes[None, :, :] == owner_ids[:, None, None]
        member = jnp.any(matches, axis=2)
        weight_tok = jnp.sum(
            jnp.where(matches, combine[None, :, :].astype(jnp.float32), 0.0), axis=2
        )
        slot_rank = jnp.cumsum(member.astype(jnp.int32), axis=1) - 1
        slot_ids = jnp.arange(slot_count, dtype=jnp.int32)
        picked_slots = member[:, None, :] & (slot_rank[:, None, :] == slot_ids[None, :, None])
        select = picked_slots.astype(jnp.bfloat16).reshape(rows, col_tok)
        weighted = jnp.where(picked_slots, weight_tok[:, None, :], 0.0)
        slot_weight = jnp.sum(weighted, axis=2).reshape(rows, 1)
        spread = weighted.astype(jnp.bfloat16).reshape(rows, col_tok)

    def over_planes(slots):
        moved = lax.all_to_all(
            slots.reshape(n_expert, slot_count, cols), "expert", 0, 0, tiled=True
        )
        return moved.reshape(rows, cols)

    def swap_in_two(pieces):
        half = LINE // 2
        crossed = [None] * LINE
        for first in range(half):
            arrived = swap_cores(jnp.concatenate(pieces[first::half]))
            crossed[first::half] = list(arrived.reshape(half, *pieces[0].shape))
        return crossed

    def place(whole, pieces, lines, other):
        for line, piece in reversed(list(zip(lines, pieces))):
            whole = lax.dynamic_update_slice_in_dim(whole, piece, first_col(line, other), 1)
        return whole

    with jax.named_scope("dispatch"):
        own_cols = columns(tokens, line_index, 0)
        outgoing = jnp.dot(select, own_cols, preferred_element_type=jnp.float32)
        arrived = over_planes(outgoing.astype(jnp.bfloat16))
        direction_other = swap_cores(
            jnp.concatenate(
                [columns(direction, line_index ^ mask, 1) for mask in range(LINE)], axis=1
            )
        )
        both = jnp.concatenate([gate_weight, up_weight], axis=0)
        arrived, direction_other, both = lax.optimization_barrier((arrived, direction_other, both))
        near_blocks = gather_line(arrived)
        row_blocks = [near_blocks, swap_in_two(near_blocks)]

    with jax.named_scope("experts"):
        value = 0.0
        for other, blocks in enumerate(row_blocks):
            for line, block in zip(gathered, blocks):
                value += lax.dot_general(
                    block,
                    columns(both, line, other),
                    (((1,), (1,)), ((), ())),
                    preferred_element_type=jnp.float32,
                )
        hidden = jax.nn.silu(value[:, :unit_count]) * value[:, unit_count:]
        hidden = hidden.astype(jnp.bfloat16)
        hidden_other = swap_cores(hidden)

    with jax.named_scope("combine"):
        def pair_out(mask):
            own = jnp.dot(
                hidden, columns(direction, line_index ^ mask, 0), preferred_element_type=jnp.float32
            )
            other = jnp.dot(
                hidden_other,
                direction_other[:, mask * cols : (mask + 1) * cols],
                preferred_element_type=jnp.float32,
            )
            return own + other

        expert_out = reduce_line([pair_out(mask) for mask in range(LINE)])
        returned = over_planes(expert_out.astype(jnp.bfloat16))
        part = contract_rows(spread, returned).astype(jnp.bfloat16)
        parts = lax.all_to_all(
            jnp.broadcast_to(part, (EXP_COL // HALVES, col_tok, cols)), "x", 0, 0, tiled=True
        )
        half = jnp.sum(parts.astype(jnp.float32), axis=0).astype(jnp.bfloat16)
        half = lax.optimization_barrier(half)
        total = half.astype(jnp.float32) + swap_halves(half).astype(jnp.float32)
        tangent_cols = total.astype(jnp.bfloat16)

    with jax.named_scope("curvature"):
        picked = jnp.dot(select, tangent_cols, preferred_element_type=jnp.float32)
        scaled = (picked * slot_weight).astype(jnp.bfloat16)
        scaled, tangent_late = lax.optimization_barrier((scaled, tangent_cols))
        moved = over_planes(scaled)

    with jax.named_scope("tangent"):
        pieces = gather_ring(tangent_late)
        moved, *pieces = lax.optimization_barrier((moved, *pieces))
        around = [line_index + step for step in (0, -1, 1, -2)]

    with jax.named_scope("curvature"):
        scaled_blocks = gather_line(moved)

    with jax.named_scope("curvature"):
        def products(units):
            return [contract_rows(units, block).astype(jnp.bfloat16) for block in scaled_blocks]

        curvature = jnp.zeros((unit_count, width), jnp.bfloat16)
        curvature = place(curvature, products(hidden), gathered, 0)
        curvature = place(curvature, swap_in_two(products(hidden_other)), gathered, 1)

    with jax.named_scope("tangent"):
        tangent_out = place(jnp.zeros((col_tok, width), jnp.bfloat16), pieces, around, 0)
        crossed = swap_cores(jnp.concatenate(pieces)).reshape(LINE, col_tok, cols)
        tangent_out = place(tangent_out, list(crossed), around, 1)
    return tangent_out, curvature


def solution(mesh):
    n_expert = mesh.shape["expert"]
    fine = Mesh(
        mesh.devices.reshape(n_expert, EXP_COL // HALVES, HALVES, LINE, CORES),
        ("expert", "x", "half", "line", "core"),
    )
    by_block = P("expert", None)
    by_device = P(("expert", "x", "half", "line", "core"), None)
    return jax.shard_map(
        shards,
        mesh=fine,
        in_specs=(by_block, by_block, by_block, by_device, by_device, by_device),
        out_specs=(by_block, by_device),
        check_vma=False,
    )
```

```python
import jax
import jax.numpy as jnp
from jax import lax
from jax.sharding import Mesh, PartitionSpec as P

TOP = 8
EXP_COL = 8
CORES = 2
LINE = 4
HALVES = 2


def contract_rows(left, right):
    return lax.dot_general(
        left, right, (((0,), (0,)), ((), ())), preferred_element_type=jnp.float32
    )


def send_line(value, pairs):
    return lax.ppermute(value, "line", pairs)


PAIRS = [(0, 1), (1, 0), (2, 3), (3, 2)]
INNER = [(1, 2), (2, 1)]
OUTWARD = [(1, 0), (2, 3)]
INWARD = [(0, 1), (3, 2)]
FAR_OUT = [(2, 0), (1, 3)]
FAR_IN = [(0, 2), (3, 1)]


def gather_line(block):
    paired = send_line(block, PAIRS)
    inner = send_line(block, INNER)
    second = inner + send_line(inner, OUTWARD)
    third = send_line(paired, INNER) + send_line(paired, FAR_OUT)
    return [block, paired, second, third]


def reduce_line(pieces):
    def send(value, pairs):
        return send_line(value.astype(jnp.bfloat16), pairs)

    far = send(pieces[3], FAR_IN)
    inner, near = send(pieces[2], INNER), send(pieces[2], INWARD)
    far, inner, near = lax.optimization_barrier((far, inner, near))
    paired, crossed = send(pieces[1] + far + inner, PAIRS), send(pieces[3] + near, INNER)
    return pieces[0] + paired + crossed


def gather_ring(block):
    ring = HALVES * LINE
    return [
        block,
        *(
            lax.ppermute(block, ("half", "line"), [(i, (i + step) % ring) for i in range(ring)])
            for step in (1, ring - 1, 2)
        ),
    ]


def swap_cores(value):
    return lax.ppermute(value, "core", [(i, i ^ 1) for i in range(CORES)])


def swap_halves(value):
    return lax.ppermute(value, "half", [(i, i ^ 1) for i in range(HALVES)])


def shards(tokens, routes, combine, gate_weight, up_weight, direction):
    n_expert = lax.axis_size("expert")
    n_slice = LINE * CORES
    col_tok, width = tokens.shape
    unit_count = gate_weight.shape[0]
    cols = width // n_slice
    slot_count = 2 * col_tok * TOP // (EXP_COL * n_expert)
    rows = n_expert * slot_count
    local_index = lax.axis_index(("x", "half"))
    line_index = lax.axis_index("line")
    core_index = lax.axis_index("core")

    is_inner = ((line_index == 1) | (line_index == 2)).astype(jnp.int32)
    gathered = [line_index ^ mask for mask in (0, 1, 2 + is_inner, 3 - is_inner)]

    def first_col(line, other):
        return ((line & (LINE - 1)) * CORES + (core_index ^ other)) * cols

    def columns(weight, line, other):
        return lax.dynamic_slice_in_dim(weight, first_col(line, other), cols, 1)

    with jax.named_scope("routing"):
        owner_ids = jnp.arange(n_expert, dtype=jnp.int32) * EXP_COL + local_index
        matches = routes[None, :, :] == owner_ids[:, None, None]
        member = jnp.any(matches, axis=2)
        weight_tok = jnp.sum(
            jnp.where(matches, combine[None, :, :].astype(jnp.float32), 0.0), axis=2
        )
        slot_rank = jnp.cumsum(member.astype(jnp.int32), axis=1) - 1
        slot_ids = jnp.arange(slot_count, dtype=jnp.int32)
        picked_slots = member[:, None, :] & (slot_rank[:, None, :] == slot_ids[None, :, None])
        select = picked_slots.astype(jnp.bfloat16).reshape(rows, col_tok)
        weighted = jnp.where(picked_slots, weight_tok[:, None, :], 0.0)
        slot_weight = jnp.sum(weighted, axis=2).reshape(rows, 1)
        spread = weighted.astype(jnp.bfloat16).reshape(rows, col_tok)

    def over_planes(slots):
        moved = lax.all_to_all(
            slots.reshape(n_expert, slot_count, cols), "expert", 0, 0, tiled=True
        )
        return moved.reshape(rows, cols)

    def swap_in_two(pieces):
        half = LINE // 2
        crossed = [None] * LINE
        for first in range(half):
            arrived = swap_cores(jnp.concatenate(pieces[first::half]))
            crossed[first::half] = list(arrived.reshape(half, *pieces[0].shape))
        return crossed

    def place(whole, pieces, lines, other):
        for line, piece in reversed(list(zip(lines, pieces))):
            whole = lax.dynamic_update_slice_in_dim(whole, piece, first_col(line, other), 1)
        return whole

    with jax.named_scope("dispatch"):
        own_cols = columns(tokens, line_index, 0)
        outgoing = jnp.dot(select, own_cols, preferred_element_type=jnp.float32)
        arrived = over_planes(outgoing.astype(jnp.bfloat16))
        direction_other = swap_cores(
            jnp.concatenate(
                [columns(direction, line_index ^ mask, 1) for mask in range(LINE)], axis=1
            )
        )
        both = jnp.concatenate([gate_weight, up_weight], axis=0)
        arrived, direction_other, both = lax.optimization_barrier((arrived, direction_other, both))
        near_blocks = gather_line(arrived)
        row_blocks = [near_blocks, swap_in_two(near_blocks)]

    with jax.named_scope("experts"):
        value = 0.0
        for other, blocks in enumerate(row_blocks):
            for line, block in zip(gathered, blocks):
                value += lax.dot_general(
                    block,
                    columns(both, line, other),
                    (((1,), (1,)), ((), ())),
                    preferred_element_type=jnp.float32,
                )
        hidden = jax.nn.silu(value[:, :unit_count]) * value[:, unit_count:]
        hidden = hidden.astype(jnp.bfloat16)
        hidden_other = swap_cores(hidden)

    with jax.named_scope("combine"):
        other_out = jnp.dot(hidden_other, direction_other, preferred_element_type=jnp.float32)

        def pair_out(mask):
            own = jnp.dot(
                hidden, columns(direction, line_index ^ mask, 0), preferred_element_type=jnp.float32
            )
            return own + other_out[:, mask * cols : (mask + 1) * cols]

        expert_out = reduce_line([pair_out(mask) for mask in range(LINE)])
        returned = over_planes(expert_out.astype(jnp.bfloat16))
        part = contract_rows(spread, returned).astype(jnp.bfloat16)
        parts = lax.all_to_all(
            jnp.broadcast_to(part, (EXP_COL // HALVES, col_tok, cols)), "x", 0, 0, tiled=True
        )
        half = jnp.sum(parts.astype(jnp.float32), axis=0).astype(jnp.bfloat16)
        half = lax.optimization_barrier(half)
        total = half.astype(jnp.float32) + swap_halves(half).astype(jnp.float32)
        tangent_cols = total.astype(jnp.bfloat16)

    with jax.named_scope("curvature"):
        picked = jnp.dot(select, tangent_cols, preferred_element_type=jnp.float32)
        scaled = (picked * slot_weight).astype(jnp.bfloat16)
        scaled, tangent_late = lax.optimization_barrier((scaled, tangent_cols))
        moved = over_planes(scaled)

    with jax.named_scope("tangent"):
        pieces = gather_ring(tangent_late)
        moved, *pieces = lax.optimization_barrier((moved, *pieces))
        around = [line_index + step for step in (0, -1, 1, -2)]

    with jax.named_scope("curvature"):
        scaled_blocks = gather_line(moved)
        scaled_blocks[1], *pieces = lax.optimization_barrier((scaled_blocks[1], *pieces))

    with jax.named_scope("curvature"):
        def products(units):
            return [contract_rows(units, block).astype(jnp.bfloat16) for block in scaled_blocks]

        curvature = jnp.zeros((unit_count, width), jnp.bfloat16)
        curvature = place(curvature, products(hidden), gathered, 0)
        curvature = place(curvature, swap_in_two(products(hidden_other)), gathered, 1)

    with jax.named_scope("tangent"):
        tangent_out = place(jnp.zeros((col_tok, width), jnp.bfloat16), pieces, around, 0)
        crossed = swap_cores(jnp.concatenate(pieces)).reshape(LINE, col_tok, cols)
        tangent_out = place(tangent_out, list(crossed), around, 1)
    return tangent_out, curvature


def solution(mesh):
    n_expert = mesh.shape["expert"]
    fine = Mesh(
        mesh.devices.reshape(n_expert, EXP_COL // HALVES, HALVES, LINE, CORES),
        ("expert", "x", "half", "line", "core"),
    )
    by_block = P("expert", None)
    by_device = P(("expert", "x", "half", "line", "core"), None)
    return jax.shard_map(
        shards,
        mesh=fine,
        in_specs=(by_block, by_block, by_block, by_device, by_device, by_device),
        out_specs=(by_block, by_device),
        check_vma=False,
    )
```
